128 devices in a mesh: dp: 8 (over y, core), vocab: 16 (over x, z).
Axes of the slice: x: 4, y: 4, z: 4, core: 2. Of those that a mesh axis runs over, the one named last changes fastest.
Arguments:
- hidden: bfloat16 [512, 3072], P(('dp', 'vocab')), may hold values from -16 to 16
- head_weight: bfloat16 [3072, 128256], P(None, ('dp', 'vocab')), may hold values from -1 to 1
- teacher: bfloat16 [512, 128256], P(('dp', 'vocab')), may hold values from -300 to 300
- row_token: int32 [512], replicated, may hold values from 0 to 511, each once
- labels: int32 [512], replicated, may hold values from 0 to 128255
Outputs:
- hidden_grad: float32 [512, 3072], P(('dp', 'vocab'))
- head_grad: float32 [3072, 128256], P(None, ('dp', 'vocab'))
- distill_loss: float32 [], replicated
The draws below stay inside these ranges and needn't reach their ends.
Inputs may be any that keep to these rules, and one draw needn't show every extreme that they name: row_token is a permutation of the 512 tokens.
All inputs are finite; a program needn't handle non-finite values.
Results may differ from the reference program's by a relative error of at most 0.0028.
Values may be sent and summed in bfloat16 or wider, within the bound.
No kernel may reach another device: no remote copies, remote signals or barrier semaphores. Data moves between devices by JAX's collectives and lax.ppermute only.
A program may use at most 128 MiB of HBM per device.

```python
import math
import jax
import jax.numpy as jnp
import numpy as np
from jax import lax

D = 3072
V = 128256
TOKENS = 512


def shared_head(key):
    return jax.random.normal(key, (D, V), jnp.float32) * (D // 9) ** (-0.5)


def draw_head_weight(key, part):
    base = shared_head(key)
    return jnp.clip(base, -1.0, 1.0).astype(jnp.bfloat16)


def draw_hidden(key, part):
    key = jax.random.fold_in(key, 2)
    keys = jax.random.split(key, 1)
    values = jnp.clip(jax.random.normal(keys[0], (TOKENS, D), jnp.float32), -5.0, 5.0)
    return jnp.clip(values, -16.0, 16.0).astype(jnp.bfloat16)


def draw_teacher(key, part):
    key = jax.random.fold_in(key, 3)
    keys = jax.random.split(key, 3)
    row_scale = jnp.exp(jax.random.uniform(keys[0], (TOKENS, 1), jnp.float32, jnp.log(0.4), jnp.log(2.5)))
    col_scale = jnp.exp(jax.random.uniform(keys[1], (1, V), jnp.float32, jnp.log(0.4), jnp.log(2.5)))
    values = jax.random.normal(keys[2], (TOKENS, V), jnp.float32) * 3.0 * row_scale * col_scale
    return jnp.clip(values, -300.0, 300.0).astype(jnp.bfloat16)


def touch_ends(result, key, low, top_value):
    longest = result.shape.index(max(result.shape))
    spots = []
    for shift in (0, 1):
        where = [jax.random.randint(jax.random.fold_in(key, axis), (), 0, length) for axis, length in enumerate(result.shape)]
        where[longest] = (where[longest] + shift) % result.shape[longest]
        spots.append(tuple(where))
    return result.at[spots[0]].set(low).at[spots[1]].set(top_value)


def skewed_wide(rng, dims, amount, lean):
    loads = [min(1 << octave, amount + 1 - (1 << octave)) * (1 << 20) // math.isqrt((1 << octave) ** lean) + 1 for octave in range((amount + 1).bit_length()) if 1 << octave <= amount]
    width = 1 + sum(loads) // (1 << 30)
    grid = np.cumsum(np.array([max(1, weight // width) for weight in loads]))
    lot = jax.random.randint(jax.random.fold_in(rng, 1), dims, 0, int(grid[len(loads) - 1]))
    start = jnp.left_shift(1, jnp.searchsorted(jnp.asarray(grid, jnp.int32), lot, side="right").astype(jnp.int32))
    grade = start - 1 + jax.random.randint(jax.random.fold_in(rng, 4), dims, 0, 1 << 30) % jnp.minimum(start, amount + 1 - start)
    return jax.random.permutation(jax.random.fold_in(rng, 2), amount)[grade].astype(jnp.int32)


def setup_inputs(seed: int = 0) -> dict:
    arg_keys = jax.random.split(jax.random.key(seed), 6)
    hidden = draw_hidden(jax.random.fold_in(arg_keys[5], 71), 0)
    head_weight = draw_head_weight(jax.random.fold_in(arg_keys[5], 71), 0)
    teacher = draw_teacher(jax.random.fold_in(arg_keys[5], 71), 0)
    row_token = jax.random.permutation(arg_keys[3], TOKENS).astype(jnp.int32)
    labels = touch_ends(skewed_wide(arg_keys[4], (TOKENS,), V, 2), jax.random.fold_in(arg_keys[4], 3), 0, V - 1).astype(jnp.int32)
    return {"hidden": hidden, "head_weight": head_weight, "teacher": teacher, "row_token": row_token, "labels": labels}


def reference(hidden, head_weight, teacher, row_token, labels):
    student = jnp.dot(hidden, head_weight, preferred_element_type=jnp.float32)
    taught = jnp.zeros_like(teacher).at[row_token].set(teacher).astype(jnp.float32)
    top_student = jnp.max(student, axis=1, keepdims=True)
    exp_student = jnp.exp(student - top_student)
    sum_student = jnp.sum(exp_student, axis=1)
    top_teacher = jnp.max(taught, axis=1, keepdims=True)
    exp_teacher = jnp.exp(taught - top_teacher)
    sum_teacher = jnp.sum(exp_teacher, axis=1)
    weighted = jnp.sum(exp_teacher * (taught - student), axis=1)
    columns = lax.iota(jnp.int32, student.shape[1])
    label_hit = labels[:, None] == columns[None, :]
    picked = jnp.sum(jnp.where(label_hit, student, 0.0), axis=1)
    lse_student = top_student[:, 0] + jnp.log(sum_student)
    lse_teacher = top_teacher[:, 0] + jnp.log(sum_teacher)
    divergence = weighted / sum_teacher - lse_teacher + lse_student
    cross = lse_student - picked
    distill_loss = jnp.mean(divergence + 0.25 * cross)
    prob_student = exp_student / sum_student[:, None]
    prob_teacher = exp_teacher / sum_teacher[:, None]
    dlogits = (64.0 * (1.25 * prob_student - prob_teacher - 0.25 * label_hit.astype(jnp.float32))).astype(jnp.bfloat16)
    head_grad = lax.dot_general(hidden, dlogits, (((0,), (0,)), ((), ())), preferred_element_type=jnp.float32)
    hidden_grad = lax.dot_general(dlogits, head_weight, (((1,), (1,)), ((), ())), preferred_element_type=jnp.float32)
    return hidden_grad, head_grad, distill_loss
```

```python
import jax
import jax.numpy as jnp
from jax import lax
from jax.experimental import pallas as pl
from jax.experimental.pallas import tpu as pltpu
from jax.sharding import Mesh, PartitionSpec as P

ALL = ("y", "core", "x", "z")
CHIPS = ("y", "x", "z")
SWAP = [(0, 1), (1, 0)]


def exchange(blocks, axes):
    return lax.all_to_all(blocks, axes, split_axis=0, concat_axis=0, tiled=True)


def spread(block, axes, count):
    return exchange(jnp.broadcast_to(block[None], (count,) + block.shape), axes)


def log_sum_exp(values, axis):
    top = jnp.max(values, axis=axis, keepdims=True)
    total = jnp.sum(jnp.exp(values - top), axis=axis)
    return jnp.squeeze(top, axis) + jnp.log(total)


def in_thirds(values):
    high = lax.reduce_precision(values, 8, 7)
    rest = values - high
    middle = lax.reduce_precision(rest, 8, 7)
    return jnp.stack([high, middle, rest - middle], axis=-1).astype(jnp.bfloat16)


def teach_kernel(offset_ref, token_ref, order_ref, label_ref, student_m_ref, student_o_ref,
                 loaded_ref, taught_m_ref, taught_o_ref, lse_ref, loss_ref):
    shard_width, half = student_m_ref.shape
    tokens = 2 * half
    pick = (token_ref[...] == order_ref[...]).astype(jnp.float32).astype(jnp.bfloat16)

    def columns(start, size):
        return lax.dot_general(
            loaded_ref[:, start : start + size],
            pick,
            (((0,), (0,)), ((), ())),
            preferred_element_type=jnp.float32,
        )

    last = shard_width // 128 * 128
    tail = columns(last, shard_width + 3 - last)
    row = lax.broadcasted_iota(jnp.int32, tail.shape, 0) + last
    lse = jnp.sum(jnp.where(row >= shard_width, tail, 0.0), axis=0, keepdims=True)
    lse_ref[...] = lse
    loss = jnp.zeros((1, tokens), jnp.float32)
    for start in range(0, shard_width, 128):
        size = min(128, shard_width - start)
        taught = tail[:size] if start == last else columns(start, size)
        at = pl.ds(start, size)
        taught_m_ref[at, :] = taught[:, :half].astype(jnp.bfloat16)
        taught_o_ref[at, :] = taught[:, half:].astype(jnp.bfloat16)
        student = jnp.concatenate([student_m_ref[at, :], student_o_ref[at, :]], axis=1)
        row = lax.broadcasted_iota(jnp.int32, (size, tokens), 0) + (start + offset_ref[0])
        term = jnp.exp(taught - lse) * (taught - student)
        term -= jnp.where(row == label_ref[...], 0.25 * student, 0.0)
        loss += jnp.sum(term, axis=0, keepdims=True)
    loss_ref[...] = sum(loss[:, k : k + 128] for k in range(0, tokens, 128))


def teach(offset, token, order, label, student_m, student_o, loaded):
    shard_width, half = student_m.shape
    tokens = 2 * half
    vmem = pl.BlockSpec(memory_space=pltpu.VMEM)
    return pl.pallas_call(
        teach_kernel,
        in_specs=[pl.BlockSpec(memory_space=pltpu.SMEM)] + [vmem] * 6,
        out_specs=[vmem] * 4,
        out_shape=[
            jax.ShapeDtypeStruct((shard_width, half), jnp.bfloat16),
            jax.ShapeDtypeStruct((shard_width, half), jnp.bfloat16),
            jax.ShapeDtypeStruct((1, tokens), jnp.float32),
            jax.ShapeDtypeStruct((1, 128), jnp.float32),
        ],
        compiler_params=pltpu.CompilerParams(vmem_limit_bytes=24 << 20),
        cost_estimate=pl.CostEstimate(
            flops=2 * shard_width * tokens * tokens,
            bytes_accessed=8 * shard_width * tokens,
            transcendentals=shard_width * tokens,
        ),
    )(offset, token, order, label, student_m, student_o, loaded)


def per_device(hidden, head_weight, teacher, row_token, labels):
    rows, width = hidden.shape
    shard_width = head_weight.shape[1]
    core = lax.axis_index("core")
    tokens = row_token.shape[0]
    half = tokens // 2
    devices = tokens // rows

    gathered = spread(hidden, CHIPS, devices // 2)

    lse_rows = in_thirds(log_sum_exp(teacher.astype(jnp.float32), 1))
    entries = teacher.reshape(rows, devices, shard_width).transpose(1, 0, 2)
    entries = jnp.concatenate(
        [entries, jnp.broadcast_to(lse_rows[None], (devices, rows, 3))], axis=2
    )
    loaded = exchange(entries, ALL)

    mine = gathered.reshape(half, width)
    other = lax.ppermute(mine, "core", SWAP)
    student_m = jnp.dot(mine, head_weight, preferred_element_type=jnp.float32)
    student_o = jnp.dot(other, head_weight, preferred_element_type=jnp.float32)
    lse_m, lse_o = log_sum_exp(student_m, 1), log_sum_exp(student_o, 1)
    loaded, student_m, student_o, lse_m, lse_o = lax.optimization_barrier(
        (loaded, student_m, student_o, lse_m, lse_o)
    )
    loaded = loaded.reshape(tokens, shard_width + 3)

    def flip(pair):
        return jnp.where(core == 0, pair, pair[::-1])

    def arranged(values):
        return flip(values.reshape(4, 2, half // 4).transpose(1, 0, 2).reshape(2, half))

    order = arranged(jnp.arange(tokens, dtype=jnp.int32))
    label_order = arranged(labels)
    first = lax.axis_index(ALL) * shard_width
    columns = first + lax.iota(jnp.int32, shard_width)
    taught_m, taught_o, lse_t, loss = teach(
        first[None],
        row_token[:, None],
        order.reshape(1, tokens),
        label_order.reshape(1, tokens),
        student_m.T,
        student_o.T,
        loaded,
    )

    stats = jnp.concatenate([flip(jnp.stack([lse_m, lse_o])).reshape(tokens), loss[0]])
    stats = spread(stats[None], ALL, devices).reshape(devices, tokens + 128)
    lse = log_sum_exp(stats[:, :tokens], 0)
    lse_t = lse_t.reshape(2, half)
    shift = flip(lse.reshape(2, half)), lse_t
    distill_loss = jnp.sum(stats[:, tokens:]) + jnp.sum(1.25 * lse.reshape(2, half) - flip(lse_t))
    distill_loss = distill_loss / tokens

    def gradient(index, student, taught):
        hit = label_order[index][:, None] == columns[None, :]
        return (
            80.0 * jnp.exp(student - shift[0][index][:, None])
            - 64.0 * jnp.exp(taught.T.astype(jnp.float32) - shift[1][index][:, None])
            - jnp.where(hit, 16.0, 0.0)
        ).astype(jnp.bfloat16)

    across = (((1,), (1,)), ((), ()))
    grad_o = gradient(1, student_o, taught_o)
    sent = lax.dot_general(grad_o, head_weight, across, preferred_element_type=jnp.float32)
    sent = sent.astype(jnp.bfloat16)
    received = lax.ppermute(sent, "core", SWAP)
    student_m, sent = lax.optimization_barrier((student_m, sent))
    grad_m = gradient(0, student_m, taught_m)
    kept = lax.dot_general(grad_m, head_weight, across, preferred_element_type=jnp.float32)
    kept, grad_m = lax.optimization_barrier((kept, grad_m))
    summed = (kept + received.astype(jnp.float32)).astype(jnp.bfloat16).reshape(devices // 2, rows, width)
    summed, grad_m, grad_o = lax.optimization_barrier((summed, grad_m, grad_o))
    pieces = exchange(summed, CHIPS)

    head_grad = lax.dot_general(
        jnp.concatenate([mine, other]),
        jnp.concatenate([grad_m, grad_o]),
        (((0,), (0,)), ((), ())),
        preferred_element_type=jnp.float32,
    )
    pieces, head_grad = lax.optimization_barrier((pieces, head_grad))
    hidden_grad = jnp.sum(pieces.astype(jnp.float32), axis=0)
    return (hidden_grad, head_grad, distill_loss)


def solution(mesh):
    grid = Mesh(mesh.devices.reshape(4, 2, 4, 4), ALL)
    in_specs = (P(ALL, None), P(None, ALL), P(ALL, None), P(), P())
    out_specs = (P(ALL, None), P(None, ALL), P())
    return jax.shard_map(
        per_device, mesh=grid, in_specs=in_specs, out_specs=out_specs, check_vma=False
    )
```
